512 devices in a mesh: tm: 32 (over z, y_lo), base: 16 (over x, y_hi, core).
Axes of the slice: x: 4, y: 8 (y_hi: 2, y_lo: 4; y = y_hi * 4 + y_lo), z: 8, core: 2. Of those that a mesh axis runs over, the one named last changes fastest.
Arguments:
- visibilities: bfloat16 [4096, 1024, 128], P('tm', 'base'), may hold values from -6 to 6
- pseudo_inverse: bfloat16 [512, 1024, 1024], P('tm', 'base'), may hold values from -0.25 to 0.25
- baseline_group: int32 [1024], P('base'), may hold values from 0 to 7
- group_count: int32 [512], P('tm'), may hold values from 4 to 8
Outputs:
- sky: bfloat16 [512, 512, 128], P('tm', 'base')
The draws below stay inside these ranges and needn't reach their ends.
All inputs are finite; a program needn't handle non-finite values.
Results may differ from the reference program's by a relative error of at most 0.0055.
Values may be sent and summed in bfloat16 or wider, within the bound.
No kernel may reach another device: no remote copies, remote signals or barrier semaphores. Data moves between devices by JAX's collectives and lax.ppermute only.
A program may use at most 64 MiB of HBM per device.

```python
import math
import jax
import jax.numpy as jnp
from jax import lax

NS = 64
L = 512
NG = 8
NT = 4096
B = 1024
NM = 512


def plant(entries, stream_key, low, top_value):
    spot = [jax.random.randint(jax.random.fold_in(stream_key, axis), (), 0, length) for axis, length in enumerate(entries.shape)]
    longest = entries.shape.index(max(entries.shape))
    beside = spot[:longest] + [(spot[longest] + 1) % entries.shape[longest]] + spot[longest + 1:]
    return entries.at[tuple(spot)].set(low).at[tuple(beside)].set(top_value)


def spiked(drawn, own_key, source, target, shards_of, factor):
    owner, partner = [(jnp.arange(drawn.shape[dim]) // (drawn.shape[dim] // shards_of)).reshape([-1 if axis == dim else 1 for axis in range(drawn.ndim)]) for dim in (source, target)]
    chosen = jax.random.permutation(own_key, shards_of)[partner]
    strong = (owner == chosen) | (owner == (partner + shards_of // 2) % shards_of)
    return jnp.where(strong, factor * drawn, drawn)


def shard_levels(key, extent, pieces, least, largest):
    loudness, own = 1.0, jax.random.fold_in(key, 6)
    for axis_at, shards_of in pieces:
        draws = jnp.exp(jax.random.uniform(jax.random.fold_in(own, axis_at), (shards_of,), jnp.float32, least / len(pieces), largest / len(pieces)))
        loudness = loudness * jnp.repeat(draws, extent[axis_at] // shards_of).reshape([-1 if axis == axis_at else 1 for axis in range(len(extent))])
    return loudness


def centred(own_key, dims, width, most, pieces=(), kind=jnp.bfloat16):
    result = jax.random.normal(own_key, dims, jnp.float32) * width
    if len(pieces) > 0:
        result = shard_levels(own_key, dims, pieces, -0.22, 0.18) * result
    return jnp.clip(result, min=-most, max=most).astype(kind)


def heavy_noise(stream_key, dims, spread, reach, shards, heavy, kind=jnp.bfloat16):
    entries = spread * jax.random.normal(stream_key, dims, jnp.float32)
    if shards:
        entries = entries * shard_levels(stream_key, dims, shards, -0.22, 0.18)
    return jnp.clip(spiked(entries, jax.random.fold_in(stream_key, 3), *heavy), -reach, reach).astype(kind)


def setup_inputs(seed: int = 0) -> dict:
    keys = jax.random.split(jax.random.key(seed), 5)
    visibilities = centred(keys[0], (NT, B, 2 * NS), 1.0, 6.0, ((0, 32), (1, 16)))
    pseudo_inverse = heavy_noise(keys[1], (NM, B, 2 * L), B ** -0.5, 0.25, ((0, 32), (1, 16)), (1, 2, 16, 2.0))
    baseline_group = plant(jax.random.randint(keys[2], (B,), 0, NG), jax.random.fold_in(keys[2], 1), 0, NG - 1).astype(jnp.int32)
    group_count = plant(jax.random.randint(keys[3], (NM,), NG // 2, NG + 1), jax.random.fold_in(keys[3], 1), NG // 2, NG).astype(jnp.int32)
    return {"visibilities": visibilities, "pseudo_inverse": pseudo_inverse, "baseline_group": baseline_group, "group_count": group_count}


def twiddles(start_position, row_entries, harmonic_orders_full, sidereal_epoch_count):
    index = start_position + jnp.arange(row_entries, dtype=jnp.int32)
    mode_value = index - harmonic_orders_full // 2
    sample_index = jnp.arange(sidereal_epoch_count, dtype=jnp.int32)
    phase_index = (mode_value % sidereal_epoch_count)[:, None] * sample_index[None, :] % sidereal_epoch_count
    angle = phase_index.astype(jnp.float32) * (2.0 * math.pi / sidereal_epoch_count)
    return (jnp.cos(angle).astype(jnp.bfloat16), jnp.sin(angle).astype(jnp.bfloat16))

def block_of_modes(correlator_data_vector, start_position, row_entries, harmonic_orders_full, sidereal_epoch_count, baseline_list, group_extent):
    cosine_term, sine_term = twiddles(start_position, row_entries, harmonic_orders_full, sidereal_epoch_count)
    times_cosine = jnp.dot(cosine_term, correlator_data_vector, preferred_element_type=jnp.float32).reshape(row_entries, baseline_list, 2 * group_extent)
    times_sine = jnp.dot(sine_term, correlator_data_vector, preferred_element_type=jnp.float32).reshape(row_entries, baseline_list, 2 * group_extent)
    real_part = times_cosine[..., :group_extent] + times_sine[..., group_extent:]
    imag_part = times_cosine[..., group_extent:] - times_sine[..., :group_extent]
    scale = 1.0 / math.sqrt(sidereal_epoch_count)
    return (jnp.concatenate([real_part, imag_part], axis=-1) * scale).astype(jnp.bfloat16)

def harmonics(inverse_rows, mode_rows):
    harm = inverse_rows.shape[2] // 2
    group_extent = mode_rows.shape[2] // 2
    product = jnp.einsum('mbk,mbs->mks', inverse_rows.astype(jnp.float32), mode_rows.astype(jnp.float32), precision=lax.Precision.HIGHEST)
    real_part = product[:, :harm, :group_extent] - product[:, harm:, group_extent:]
    imag_part = product[:, :harm, group_extent:] + product[:, harm:, :group_extent]
    return jnp.concatenate([real_part, imag_part], axis=-1)

def reference(visibilities, pseudo_inverse, baseline_group, group_count):
    correlator_data_vector = visibilities.reshape(NT, B * 2 * NS)
    rows_per_block = 128
    start_positions = jnp.arange(NM // rows_per_block, dtype=jnp.int32) * rows_per_block

    def single_block(start_position):
        return block_of_modes(correlator_data_vector, start_position, rows_per_block, NM, NT, B, NS)
    mode_list = lax.map(single_block, start_positions).reshape(NM, B, 2 * NS)
    active = (baseline_group[None, :] < group_count[:, None]).astype(jnp.bfloat16)
    masked = pseudo_inverse * active[:, :, None]
    beam_rows = 16
    masked_blocks = masked.reshape(NM // beam_rows, beam_rows, B, 2 * L)
    harmonic_tiles = mode_list.reshape(NM // beam_rows, beam_rows, B, 2 * NS)

    def beam_block(pair):
        return harmonics(pair[0], pair[1]).astype(jnp.bfloat16)
    sky = lax.map(beam_block, (masked_blocks, harmonic_tiles))
    return sky.reshape(NM, L, 2 * NS)
```

```python
import functools
import math

import jax
import jax.numpy as jnp
import ml_dtypes
import numpy as np
from jax import lax
from jax.experimental import pallas as pl
from jax.experimental.pallas import tpu as pltpu
from jax.sharding import Mesh, PartitionSpec as P

MIB = 1 << 20


def tables(modes, samples):
    half = modes // 2
    t = np.arange(samples // 4, dtype=np.int64)
    k = np.arange(half + 1, dtype=np.int64)[:, None] * t[None, :] % samples
    angle = np.arange(samples, dtype=np.float64) * (2.0 * math.pi / samples)
    cosine = np.cos(angle).astype(np.float32).astype(ml_dtypes.bfloat16)[k]
    sine = np.sin(angle).astype(np.float32).astype(ml_dtypes.bfloat16)[k]
    rest = np.zeros((14, samples // 4), ml_dtypes.bfloat16)
    return np.concatenate([cosine[:half], sine[:half], cosine[half:], sine[half:], rest])


def permutation(order):
    matrix = np.zeros((len(order), len(order)), ml_dtypes.bfloat16)
    matrix[np.arange(len(order)), order] = 1
    return matrix


def whole():
    return pl.BlockSpec(memory_space=pltpu.VMEM)


def by_baseline(visibilities):
    times, baselines, width = visibilities.shape
    half, tile, block = baselines // 2, 16, 32
    blocks = times // block

    def kernel(in_ref, out_ref, near, turned, in_sems, out_sems):
        def fetch(i):
            at = pl.ds(i * block, block)
            return pltpu.make_async_copy(in_ref.at[at], near.at[at], in_sems.at[i])

        def store(i):
            at = pl.ds(i * block, block)
            return pltpu.make_async_copy(
                turned.at[:, at, :], out_ref.at[:, at, :], out_sems.at[i]
            )

        for i in range(blocks):
            fetch(i).start()
        for i in range(blocks):
            fetch(i).wait()
            for t in range(i * block, (i + 1) * block, tile):
                for b in range(0, baselines, tile):
                    rows = jnp.swapaxes(near[t : t + tile, b : b + tile, :], 0, 1)
                    h, d = divmod(b, half)
                    turned[d : d + tile, t : t + tile, h * width : (h + 1) * width] = rows
            store(i).start()
        for i in range(blocks):
            store(i).wait()

    out = (half, times, 2 * width)
    return pl.pallas_call(
        kernel,
        in_specs=[pl.BlockSpec(memory_space=pl.ANY)],
        out_specs=pl.BlockSpec(memory_space=pl.ANY),
        out_shape=jax.ShapeDtypeStruct(out, jnp.bfloat16),
        scratch_shapes=[
            pltpu.VMEM(visibilities.shape, jnp.bfloat16),
            pltpu.VMEM(out, jnp.bfloat16),
            pltpu.SemaphoreType.DMA((blocks,)),
            pltpu.SemaphoreType.DMA((blocks,)),
        ],
        compiler_params=pltpu.CompilerParams(vmem_limit_bytes=56 * MIB),
        cost_estimate=pl.CostEstimate(
            flops=0, bytes_accessed=4 * visibilities.size, transcendentals=0
        ),
        name="by_baseline",
    )(visibilities)


def prepare(blocks):
    each_m, baselines, width = blocks[0].shape
    harm, peers = width // 2, len(blocks)
    depth = 2 * peers * baselines

    def kernel(*refs):
        block_refs, inverse_ref = refs[:peers], refs[peers]
        for m in range(each_m):
            for part in range(2):
                at = slice(part * harm, (part + 1) * harm)
                for p in range(0, peers, 2):
                    two = [block_refs[p + i][m, :, at] for i in range(2)]
                    to = (part * peers + p) * baselines
                    inverse_ref[m, :, to : to + 2 * baselines] = jnp.concatenate(two, axis=0).T

    return pl.pallas_call(
        kernel,
        in_specs=[whole()] * peers,
        out_specs=whole(),
        out_shape=pltpu.VMEM((each_m, harm, depth), jnp.bfloat16),
        compiler_params=pltpu.CompilerParams(vmem_limit_bytes=12 * MIB),
        cost_estimate=pl.CostEstimate(
            flops=0, bytes_accessed=4 * each_m * harm * depth, transcendentals=0
        ),
        name="prepare",
    )(*blocks)


def transform(data, modes, ns):
    samples, width = data.shape
    quarter, half = samples // 4, modes // 2
    scale = 1.0 / math.sqrt(samples)
    table = tables(modes, samples)

    def turn(v):
        parts = []
        for b in range(0, width, 2 * ns):
            parts += [v[:, b + ns : b + 2 * ns], -v[:, b : b + ns]]
        return jnp.concatenate(parts, axis=1)

    def kernel(table_ref, data_ref, out_ref):
        z = [
            jnp.dot(
                table_ref[...],
                data_ref[j * quarter : (j + 1) * quarter, :],
                preferred_element_type=jnp.float32,
            )
            for j in range(4)
        ]
        c = [v[:half] for v in z]
        s = [v[half : 2 * half] for v in z]
        row = lax.broadcasted_iota(jnp.int32, (half, width), 0)
        odd = row % 2 == 1
        sign = jnp.where(odd, -1.0, 1.0)
        late = jnp.where(row % 4 >= 2, -1.0, 1.0)
        p_c, p_s = c[1] + sign * c[3], s[1] + sign * s[3]
        u = c[0] + sign * c[2] + late * jnp.where(odd, -p_s, p_c)
        v = turn(s[0] + sign * s[2] + late * jnp.where(odd, p_c, p_s))
        plus, minus = (u + v) * scale, (u - v) * scale
        last = z[0][2 * half :] + z[1][2 * half :] + z[2][2 * half :] + z[3][2 * half :]
        last = (last[0:1] - turn(last[1:2])) * scale
        minus = jnp.where(row == 0, last, minus).astype(jnp.bfloat16)
        both = sum(lax.broadcasted_iota(jnp.int32, (half, half), d) for d in (0, 1))
        back = jnp.where(both % half == 0, 1.0, 0.0).astype(jnp.bfloat16)
        out_ref[:half, :] = jnp.dot(
            back, minus, preferred_element_type=jnp.float32
        ).astype(jnp.bfloat16)
        out_ref[half:, :] = plus.astype(jnp.bfloat16)

    return pl.pallas_call(
        kernel,
        in_specs=[whole()] * 2,
        out_specs=whole(),
        out_shape=jax.ShapeDtypeStruct((modes, width), jnp.bfloat16),
        compiler_params=pltpu.CompilerParams(vmem_limit_bytes=12 * MIB),
        cost_estimate=pl.CostEstimate(
            flops=2 * table.size * 4 * width,
            bytes_accessed=2 * table.size + 2 * data.size,
            transcendentals=0,
        ),
        name="transform",
    )(table, data)


def product(inverse, rows, sources, devices, ns):
    each_m, harm, _ = inverse.shape
    n_rows, width = rows.shape
    peers = sources.shape[0]
    outer = n_rows // (each_m * peers)
    order = np.arange(n_rows).reshape(outer, peers, each_m).transpose(2, 1, 0).reshape(-1)
    per = harm // devices

    def kernel(sources_ref, turn_ref, rows_ref, inverse_ref, out_ref, sorted_rows):
        sorted_rows[...] = jnp.dot(
            turn_ref[...], rows_ref[...], preferred_element_type=jnp.float32
        )
        for m in range(each_m):
            plain, turned = [], []
            for p in range(peers):
                at = pl.multiple_of((m * peers + sources_ref[p]) * outer, outer)
                for h in range(0, width, 2 * ns):
                    one = sorted_rows[pl.ds(at, outer), h : h + 2 * ns]
                    plain.append(one)
                    turned.append(jnp.concatenate([-one[:, ns:], one[:, :ns]], axis=1))
            weights = jnp.concatenate(plain + turned, axis=0).astype(jnp.bfloat16)
            sky = jnp.dot(inverse_ref[m], weights, preferred_element_type=jnp.float32)
            out_ref[:, m] = sky.astype(jnp.bfloat16).reshape(devices, per, 2 * ns)

    return pl.pallas_call(
        kernel,
        in_specs=[
            pl.BlockSpec(memory_space=pltpu.SMEM),
            whole(),
            whole(),
            whole(),
        ],
        out_specs=whole(),
        out_shape=jax.ShapeDtypeStruct((devices, each_m, per, 2 * ns), jnp.bfloat16),
        scratch_shapes=[
            pltpu.VMEM((n_rows, width), jnp.float32),
        ],
        compiler_params=pltpu.CompilerParams(vmem_limit_bytes=12 * MIB),
        cost_estimate=pl.CostEstimate(
            flops=4 * inverse.size * ns, bytes_accessed=2 * inverse.size, transcendentals=0
        ),
        name="product",
    )(sources, permutation(order), rows, inverse)


def per_device(visibilities, pseudo_inverse, baseline_group, group_count):
    tm, nx, nh, nc = (lax.axis_size(a) for a in ("tm", "x", "h", "c"))
    peers = nx * nc
    x, c = lax.axis_index("x"), lax.axis_index("c")
    local_t, local_b, width = visibilities.shape
    samples = local_t * tm
    mine_m = group_count.shape[0]
    modes = mine_m * tm
    each_m = mine_m // peers
    ns = width // 2

    data = by_baseline(visibilities)
    data = lax.all_to_all(data, "tm", split_axis=0, concat_axis=0, tiled=True)
    data = data.reshape(samples, 2 * width)

    active = (baseline_group[None, :] < group_count[:, None]).astype(jnp.bfloat16)
    masked = pseudo_inverse * active[:, :, None]
    blocks, sources = [], []
    for dx in range(nx):
        for dc in range(nc):
            to = (x + dx) % nx * nc + (c + dc) % nc
            block = lax.dynamic_slice_in_dim(masked, to * each_m, each_m, 0)
            if dx or dc:
                moves = [
                    (i, (i // nc + dx) % nx * nc + (i % nc + dc) % nc) for i in range(peers)
                ]
                block = lax.ppermute(block, ("x", "c"), moves)
            blocks.append(block)
            sources.append((x - dx) % nx * nc + (c - dc) % nc)
    inverse, data = lax.optimization_barrier((prepare(blocks), data))
    rows = transform(data, modes, ns)

    rows = lax.all_to_all(rows, ("tm", "x", "c"), split_axis=0, concat_axis=0, tiled=True)
    sky = product(inverse, rows, jnp.stack(sources), nx * nh * nc, ns)

    sky = lax.all_to_all(sky, ("x", "h", "c"), split_axis=0, concat_axis=0, tiled=True)
    sky = sky.reshape(nx, nh, nc, each_m, -1, width).astype(jnp.float32).sum(axis=1)
    return sky.reshape(mine_m, -1, width).astype(jnp.bfloat16)


def solution(mesh):
    tm, base = mesh.devices.shape
    fine = Mesh(mesh.devices.reshape(tm, base // 4, 2, 2), ("tm", "x", "h", "c"))
    b = ("x", "h", "c")
    in_specs = (P("tm", b, None), P("tm", b, None), P(b), P("tm"))
    return jax.shard_map(
        per_device, mesh=fine, in_specs=in_specs, out_specs=P("tm", b, None), check_vma=False
    )
```

```python
import functools
import math

import jax
import jax.numpy as jnp
import ml_dtypes
import numpy as np
from jax import lax
from jax.experimental import pallas as pl
from jax.experimental.pallas import tpu as pltpu
from jax.sharding import Mesh, PartitionSpec as P

MIB = 1 << 20


def tables(modes, samples):
    half = modes // 2
    t = np.arange(samples // 4, dtype=np.int64)
    k = np.arange(half + 1, dtype=np.int64)[:, None] * t[None, :] % samples
    angle = np.arange(samples, dtype=np.float64) * (2.0 * math.pi / samples)
    cosine = np.cos(angle).astype(np.float32).astype(ml_dtypes.bfloat16)[k]
    sine = np.sin(angle).astype(np.float32).astype(ml_dtypes.bfloat16)[k]
    rest = np.zeros((14, samples // 4), ml_dtypes.bfloat16)
    return np.concatenate([cosine[:half], sine[:half], cosine[half:], sine[half:], rest])


def whole():
    return pl.BlockSpec(memory_space=pltpu.VMEM)


def by_baseline(visibilities):
    times, baselines, width = visibilities.shape
    half, tile, block = baselines // 2, 16, 32
    blocks = times // block

    def kernel(in_ref, out_ref, near, turned, in_sems, out_sems):
        def fetch(i):
            at = pl.ds(i * block, block)
            return pltpu.make_async_copy(in_ref.at[at], near.at[at], in_sems.at[i])

        def store(i):
            at = pl.ds(i * block, block)
            return pltpu.make_async_copy(
                turned.at[:, at, :], out_ref.at[:, at, :], out_sems.at[i]
            )

        for i in range(blocks):
            fetch(i).start()
        for i in range(blocks):
            fetch(i).wait()
            for t in range(i * block, (i + 1) * block, tile):
                for b in range(0, baselines, tile):
                    rows = jnp.swapaxes(near[t : t + tile, b : b + tile, :], 0, 1)
                    h, d = divmod(b, half)
                    turned[d : d + tile, t : t + tile, h * width : (h + 1) * width] = rows
            store(i).start()
        for i in range(blocks):
            store(i).wait()

    out = (half, times, 2 * width)
    return pl.pallas_call(
        kernel,
        in_specs=[pl.BlockSpec(memory_space=pl.ANY)],
        out_specs=pl.BlockSpec(memory_space=pl.ANY),
        out_shape=jax.ShapeDtypeStruct(out, jnp.bfloat16),
        scratch_shapes=[
            pltpu.VMEM(visibilities.shape, jnp.bfloat16),
            pltpu.VMEM(out, jnp.bfloat16),
            pltpu.SemaphoreType.DMA((blocks,)),
            pltpu.SemaphoreType.DMA((blocks,)),
        ],
        compiler_params=pltpu.CompilerParams(vmem_limit_bytes=56 * MIB),
        cost_estimate=pl.CostEstimate(
            flops=0, bytes_accessed=4 * visibilities.size, transcendentals=0
        ),
        name="by_baseline",
    )(visibilities)


def prepare(blocks, after):
    each_m, baselines, width = blocks[0].shape
    harm, peers = width // 2, len(blocks)
    depth = 2 * peers * baselines

    def kernel(*refs):
        block_refs, inverse_ref = refs[:peers], refs[peers + 1]
        for m in range(each_m):
            for part in range(2):
                at = slice(part * harm, (part + 1) * harm)
                for p in range(0, peers, 2):
                    two = [block_refs[p + i][m, :, at] for i in range(2)]
                    to = (part * peers + p) * baselines
                    inverse_ref[m, :, to : to + 2 * baselines] = jnp.concatenate(two, axis=0).T

    return pl.pallas_call(
        kernel,
        in_specs=[whole()] * peers + [pl.BlockSpec(memory_space=pl.ANY)],
        out_specs=whole(),
        out_shape=pltpu.VMEM((each_m, harm, depth), jnp.bfloat16),
        compiler_params=pltpu.CompilerParams(vmem_limit_bytes=56 * MIB),
        cost_estimate=pl.CostEstimate(
            flops=0, bytes_accessed=4 * each_m * harm * depth, transcendentals=0
        ),
        name="prepare",
    )(*blocks, after)


def transform(data, modes, ns):
    samples, width = data.shape
    quarter, half = samples // 4, modes // 2
    scale = 1.0 / math.sqrt(samples)
    table = tables(modes, samples)

    def turn(v):
        parts = []
        for b in range(0, width, 2 * ns):
            parts += [v[:, b + ns : b + 2 * ns], -v[:, b : b + ns]]
        return jnp.concatenate(parts, axis=1)

    def kernel(table_ref, data_ref, out_ref):
        z = [
            jnp.dot(
                table_ref[...],
                data_ref[j * quarter : (j + 1) * quarter, :],
                preferred_element_type=jnp.float32,
            )
            for j in range(4)
        ]
        c = [v[:half] for v in z]
        s = [v[half : 2 * half] for v in z]
        row = lax.broadcasted_iota(jnp.int32, (half, width), 0)
        odd = row % 2 == 1
        sign = jnp.where(odd, -1.0, 1.0)
        late = jnp.where(row % 4 >= 2, -1.0, 1.0)
        p_c, p_s = c[1] + sign * c[3], s[1] + sign * s[3]
        u = c[0] + sign * c[2] + late * jnp.where(odd, -p_s, p_c)
        v = turn(s[0] + sign * s[2] + late * jnp.where(odd, p_c, p_s))
        plus, minus = (u + v) * scale, (u - v) * scale
        last = z[0][2 * half :] + z[1][2 * half :] + z[2][2 * half :] + z[3][2 * half :]
        last = (last[0:1] - turn(last[1:2])) * scale
        minus = jnp.where(row == 0, last, minus).astype(jnp.bfloat16)
        both = sum(lax.broadcasted_iota(jnp.int32, (half, half), d) for d in (0, 1))
        back = jnp.where(both % half == 0, 1.0, 0.0).astype(jnp.bfloat16)
        out_ref[:half, :] = jnp.dot(
            back, minus, preferred_element_type=jnp.float32
        ).astype(jnp.bfloat16)
        out_ref[half:, :] = plus.astype(jnp.bfloat16)

    return pl.pallas_call(
        kernel,
        in_specs=[whole()] * 2,
        out_specs=whole(),
        out_shape=jax.ShapeDtypeStruct((modes, width), jnp.bfloat16),
        compiler_params=pltpu.CompilerParams(vmem_limit_bytes=12 * MIB),
        cost_estimate=pl.CostEstimate(
            flops=2 * table.size * 4 * width,
            bytes_accessed=2 * table.size + 2 * data.size,
            transcendentals=0,
        ),
        name="transform",
    )(table, data)


def product(inverse, rows, sources, devices, ns):
    each_m, harm, _ = inverse.shape
    n_rows, width = rows.shape
    peers = sources.shape[0]
    outer = n_rows // (each_m * peers)
    bits = [n.bit_length() - 1 for n in (outer, peers)]
    per = harm // devices

    def kernel(sources_ref, rows_ref, inverse_ref, out_ref, sorted_rows):
        to = lax.broadcasted_iota(jnp.int32, (n_rows, 1), 0)
        o, p, m = to & (outer - 1), (to >> bits[0]) & (peers - 1), to >> (bits[0] + bits[1])
        source = (o * peers + p) * each_m + m
        column = lax.broadcasted_iota(jnp.int32, (n_rows, n_rows), 1)
        matrix = jnp.where(column == source, 1.0, 0.0).astype(jnp.bfloat16)
        sorted_rows[...] = jnp.dot(matrix, rows_ref[...], preferred_element_type=jnp.float32)
        for m in range(each_m):
            plain, turned = [], []
            for p in range(peers):
                at = pl.multiple_of((m * peers + sources_ref[p]) * outer, outer)
                for h in range(0, width, 2 * ns):
                    one = sorted_rows[pl.ds(at, outer), h : h + 2 * ns]
                    plain.append(one)
                    turned.append(jnp.concatenate([-one[:, ns:], one[:, :ns]], axis=1))
            weights = jnp.concatenate(plain + turned, axis=0).astype(jnp.bfloat16)
            sky = jnp.dot(inverse_ref[m], weights, preferred_element_type=jnp.float32)
            out_ref[:, m] = sky.astype(jnp.bfloat16).reshape(devices, per, 2 * ns)

    return pl.pallas_call(
        kernel,
        in_specs=[
            pl.BlockSpec(memory_space=pltpu.SMEM),
            whole(),
            whole(),
        ],
        out_specs=whole(),
        out_shape=jax.ShapeDtypeStruct((devices, each_m, per, 2 * ns), jnp.bfloat16),
        scratch_shapes=[
            pltpu.VMEM((n_rows, width), jnp.float32),
        ],
        compiler_params=pltpu.CompilerParams(vmem_limit_bytes=12 * MIB),
        cost_estimate=pl.CostEstimate(
            flops=4 * inverse.size * ns, bytes_accessed=2 * inverse.size, transcendentals=0
        ),
        name="product",
    )(sources, rows, inverse)


def per_device(visibilities, pseudo_inverse, baseline_group, group_count):
    tm, nx, nh, nc = (lax.axis_size(a) for a in ("tm", "x", "h", "c"))
    peers = nx * nc
    x, c = lax.axis_index("x"), lax.axis_index("c")
    local_t, local_b, width = visibilities.shape
    samples = local_t * tm
    mine_m = group_count.shape[0]
    modes = mine_m * tm
    each_m = mine_m // peers
    ns = width // 2

    data = by_baseline(visibilities)
    data = lax.all_to_all(data, "tm", split_axis=0, concat_axis=0, tiled=True)
    data = data.reshape(samples, 2 * width)

    active = (baseline_group[None, :] < group_count[:, None]).astype(jnp.bfloat16)
    masked = pseudo_inverse * active[:, :, None]
    blocks, sources = [], []
    for dx in range(nx):
        for dc in range(nc):
            to = (x + dx) % nx * nc + (c + dc) % nc
            block = lax.dynamic_slice_in_dim(masked, to * each_m, each_m, 0)
            if dx or dc:
                moves = [
                    (i, (i // nc + dx) % nx * nc + (i % nc + dc) % nc) for i in range(peers)
                ]
                block = lax.ppermute(block, ("x", "c"), moves)
            blocks.append(block)
            sources.append((x - dx) % nx * nc + (c - dc) % nc)
    data, *blocks = lax.optimization_barrier((data, *blocks))
    rows = transform(data, modes, ns)
    inverse = prepare(blocks, rows)

    rows = lax.all_to_all(rows, ("tm", "x", "c"), split_axis=0, concat_axis=0, tiled=True)
    sky = product(inverse, rows, jnp.stack(sources), nx * nh * nc, ns)

    sky = lax.all_to_all(sky, ("x", "h", "c"), split_axis=0, concat_axis=0, tiled=True)
    sky = sky.reshape(nx, nh, nc, each_m, -1, width).astype(jnp.float32).sum(axis=1)
    return sky.reshape(mine_m, -1, width).astype(jnp.bfloat16)


def solution(mesh):
    tm, base = mesh.devices.shape
    fine = Mesh(mesh.devices.reshape(tm, base // 4, 2, 2), ("tm", "x", "h", "c"))
    b = ("x", "h", "c")
    in_specs = (P("tm", b, None), P("tm", b, None), P(b), P("tm"))
    return jax.shard_map(
        per_device, mesh=fine, in_specs=in_specs, out_specs=P("tm", b, None), check_vma=False
    )
```

```python
import functools
import math

import jax
import jax.numpy as jnp
import ml_dtypes
import numpy as np
from jax import lax
from jax.experimental import pallas as pl
from jax.experimental.pallas import tpu as pltpu
from jax.sharding import Mesh, PartitionSpec as P

MIB = 1 << 20


def tables(modes, samples):
    half = modes // 2
    t = np.arange(samples // 4, dtype=np.int64)
    k = np.arange(half + 1, dtype=np.int64)[:, None] * t[None, :] % samples
    angle = np.arange(samples, dtype=np.float64) * (2.0 * math.pi / samples)
    cosine = np.cos(angle).astype(np.float32).astype(ml_dtypes.bfloat16)[k]
    sine = np.sin(angle).astype(np.float32).astype(ml_dtypes.bfloat16)[k]
    rest = np.zeros((14, samples // 4), ml_dtypes.bfloat16)
    return np.concatenate([cosine[:half], sine[:half], cosine[half:], sine[half:], rest])


def whole():
    return pl.BlockSpec(memory_space=pltpu.VMEM)


def by_baseline(visibilities):
    times, baselines, width = visibilities.shape
    half, tile, block = baselines // 2, 16, 32
    blocks = times // block

    def kernel(in_ref, out_ref, near, turned, in_sems, out_sems):
        def fetch(i):
            at = pl.ds(i * block, block)
            return pltpu.make_async_copy(in_ref.at[at], near.at[at], in_sems.at[i])

        def store(i):
            at = pl.ds(i * block, block)
            return pltpu.make_async_copy(
                turned.at[:, at, :], out_ref.at[:, at, :], out_sems.at[i]
            )

        for i in range(blocks):
            fetch(i).start()
        for i in range(blocks):
            fetch(i).wait()
            for t in range(i * block, (i + 1) * block, tile):
                for b in range(0, baselines, tile):
                    rows = jnp.swapaxes(near[t : t + tile, b : b + tile, :], 0, 1)
                    h, d = divmod(b, half)
                    turned[d : d + tile, t : t + tile, h * width : (h + 1) * width] = rows
            store(i).start()
        for i in range(blocks):
            store(i).wait()

    out = (half, times, 2 * width)
    return pl.pallas_call(
        kernel,
        in_specs=[pl.BlockSpec(memory_space=pl.ANY)],
        out_specs=pl.BlockSpec(memory_space=pl.ANY),
        out_shape=jax.ShapeDtypeStruct(out, jnp.bfloat16),
        scratch_shapes=[
            pltpu.VMEM(visibilities.shape, jnp.bfloat16),
            pltpu.VMEM(out, jnp.bfloat16),
            pltpu.SemaphoreType.DMA((blocks,)),
            pltpu.SemaphoreType.DMA((blocks,)),
        ],
        compiler_params=pltpu.CompilerParams(vmem_limit_bytes=56 * MIB),
        cost_estimate=pl.CostEstimate(
            flops=0, bytes_accessed=4 * visibilities.size, transcendentals=0
        ),
        name="by_baseline",
    )(visibilities)


def prepare(blocks, after):
    each_m, baselines, width = blocks[0].shape
    harm, peers = width // 2, len(blocks)
    depth = 2 * peers * baselines

    def kernel(*refs):
        block_refs, inverse_ref = refs[:peers], refs[peers + 1]
        for m in range(each_m):
            for part in range(2):
                at = slice(part * harm, (part + 1) * harm)
                for p in range(0, peers, 2):
                    two = [block_refs[p + i][m, :, at] for i in range(2)]
                    to = (part * peers + p) * baselines
                    inverse_ref[m, :, to : to + 2 * baselines] = jnp.concatenate(two, axis=0).T

    return pl.pallas_call(
        kernel,
        in_specs=[whole()] * peers + [pl.BlockSpec(memory_space=pl.ANY)],
        out_specs=whole(),
        out_shape=pltpu.VMEM((each_m, harm, depth), jnp.bfloat16),
        compiler_params=pltpu.CompilerParams(vmem_limit_bytes=56 * MIB),
        cost_estimate=pl.CostEstimate(
            flops=0, bytes_accessed=4 * each_m * harm * depth, transcendentals=0
        ),
        name="prepare",
    )(*blocks, after)


def transform(data, modes, ns):
    samples, width = data.shape
    per_b = width // (2 * ns)
    quarter, half = samples // 4, modes // 2
    scale = 1.0 / math.sqrt(samples)
    table = tables(modes, samples)

    def turn(v):
        parts = []
        for b in range(0, width, 2 * ns):
            parts += [v[:, b + ns : b + 2 * ns], -v[:, b : b + ns]]
        return jnp.concatenate(parts, axis=1)

    def kernel(table_ref, data_ref, out_ref, wide):
        z = [
            jnp.dot(
                table_ref[...],
                data_ref[j * quarter : (j + 1) * quarter, :],
                preferred_element_type=jnp.float32,
            )
            for j in range(4)
        ]
        c = [v[:half] for v in z]
        s = [v[half : 2 * half] for v in z]
        row = lax.broadcasted_iota(jnp.int32, (half, width), 0)
        odd = row % 2 == 1
        sign = jnp.where(odd, -1.0, 1.0)
        late = jnp.where(row % 4 >= 2, -1.0, 1.0)
        p_c, p_s = c[1] + sign * c[3], s[1] + sign * s[3]
        u = c[0] + sign * c[2] + late * jnp.where(odd, -p_s, p_c)
        v = turn(s[0] + sign * s[2] + late * jnp.where(odd, p_c, p_s))
        plus, minus = (u + v) * scale, (u - v) * scale
        last = z[0][2 * half :] + z[1][2 * half :] + z[2][2 * half :] + z[3][2 * half :]
        last = (last[0:1] - turn(last[1:2])) * scale
        minus = jnp.where(row == 0, last, minus).astype(jnp.bfloat16)
        both = sum(lax.broadcasted_iota(jnp.int32, (half, half), d) for d in (0, 1))
        back = jnp.where(both % half == 0, 1.0, 0.0).astype(jnp.bfloat16)
        minus = jnp.dot(back, minus, preferred_element_type=jnp.float32)
        for i, value in enumerate((minus, plus)):
            for b in range(per_b):
                to = pl.ds(i * half * per_b + b, half, stride=per_b)
                wide[to, :] = value[:, b * 2 * ns : (b + 1) * 2 * ns]
        out_ref[...] = wide[...].astype(jnp.bfloat16)

    return pl.pallas_call(
        kernel,
        in_specs=[whole()] * 2,
        out_specs=whole(),
        out_shape=jax.ShapeDtypeStruct((modes * per_b, 2 * ns), jnp.bfloat16),
        scratch_shapes=[pltpu.VMEM((modes * per_b, 2 * ns), jnp.float32)],
        compiler_params=pltpu.CompilerParams(vmem_limit_bytes=12 * MIB),
        cost_estimate=pl.CostEstimate(
            flops=2 * table.size * 4 * width,
            bytes_accessed=2 * table.size + 2 * data.size,
            transcendentals=0,
        ),
        name="transform",
    )(table, data)


def product(inverse, rows, sources, devices, ns):
    each_m, harm, _ = inverse.shape
    n_rows, width = rows.shape
    peers, per_b = sources.shape[0], 2
    step = peers * each_m * per_b
    outer = n_rows // step
    per = harm // devices

    def kernel(sources_ref, rows_ref, inverse_ref, out_ref, wide):
        wide[...] = rows_ref[...].astype(jnp.float32)
        for m in range(each_m):
            plain, turned = [], []
            for p in range(peers):
                for b in range(per_b):
                    start = (sources_ref[p] * each_m + m) * per_b + b
                    one = wide[pl.ds(start, outer, stride=step), :]
                    plain.append(one)
                    turned.append(jnp.concatenate([-one[:, ns:], one[:, :ns]], axis=1))
            weights = jnp.concatenate(plain + turned, axis=0).astype(jnp.bfloat16)
            sky = jnp.dot(inverse_ref[m], weights, preferred_element_type=jnp.float32)
            out_ref[:, m] = sky.astype(jnp.bfloat16).reshape(devices, per, 2 * ns)

    return pl.pallas_call(
        kernel,
        in_specs=[
            pl.BlockSpec(memory_space=pltpu.SMEM),
            whole(),
            whole(),
        ],
        out_specs=whole(),
        out_shape=jax.ShapeDtypeStruct((devices, each_m, per, 2 * ns), jnp.bfloat16),
        scratch_shapes=[
            pltpu.VMEM((n_rows, width), jnp.float32),
        ],
        compiler_params=pltpu.CompilerParams(vmem_limit_bytes=12 * MIB),
        cost_estimate=pl.CostEstimate(
            flops=4 * inverse.size * ns, bytes_accessed=2 * inverse.size, transcendentals=0
        ),
        name="product",
    )(sources, rows, inverse)


def per_device(visibilities, pseudo_inverse, baseline_group, group_count):
    tm, nx, nh, nc = (lax.axis_size(a) for a in ("tm", "x", "h", "c"))
    peers = nx * nc
    x, c = lax.axis_index("x"), lax.axis_index("c")
    local_t, local_b, width = visibilities.shape
    samples = local_t * tm
    mine_m = group_count.shape[0]
    modes = mine_m * tm
    each_m = mine_m // peers
    ns = width // 2

    data = by_baseline(visibilities)
    data = lax.all_to_all(data, "tm", split_axis=0, concat_axis=0, tiled=True)
    data = data.reshape(samples, 2 * width)

    active = (baseline_group[None, :] < group_count[:, None]).astype(jnp.bfloat16)
    masked = pseudo_inverse * active[:, :, None]
    blocks, sources = [], []
    for dx in range(nx):
        for dc in range(nc):
            to = (x + dx) % nx * nc + (c + dc) % nc
            block = lax.dynamic_slice_in_dim(masked, to * each_m, each_m, 0)
            if dx or dc:
                moves = [
                    (i, (i // nc + dx) % nx * nc + (i % nc + dc) % nc) for i in range(peers)
                ]
                block = lax.ppermute(block, ("x", "c"), moves)
            blocks.append(block)
            sources.append((x - dx) % nx * nc + (c - dc) % nc)
    data, *blocks = lax.optimization_barrier((data, *blocks))
    rows = transform(data, modes, ns)
    inverse = prepare(blocks, rows)

    rows = lax.all_to_all(rows, ("tm", "x", "c"), split_axis=0, concat_axis=0, tiled=True)
    sky = product(inverse, rows, jnp.stack(sources), nx * nh * nc, ns)

    sky = lax.all_to_all(sky, ("x", "h", "c"), split_axis=0, concat_axis=0, tiled=True)
    sky = sky.reshape(nx, nh, nc, each_m, -1, width).astype(jnp.float32).sum(axis=1)
    return sky.reshape(mine_m, -1, width).astype(jnp.bfloat16)


def solution(mesh):
    tm, base = mesh.devices.shape
    fine = Mesh(mesh.devices.reshape(tm, base // 4, 2, 2), ("tm", "x", "h", "c"))
    b = ("x", "h", "c")
    in_specs = (P("tm", b, None), P("tm", b, None), P(b), P("tm"))
    return jax.shard_map(
        per_device, mesh=fine, in_specs=in_specs, out_specs=P("tm", b, None), check_vma=False
    )
```

```python
import functools
import math

import jax
import jax.numpy as jnp
import ml_dtypes
import numpy as np
from jax import lax
from jax.experimental import pallas as pl
from jax.experimental.pallas import tpu as pltpu
from jax.sharding import Mesh, PartitionSpec as P

MIB = 1 << 20


def tables(modes, samples):
    half = modes // 2
    t = np.arange(samples // 4, dtype=np.int64)
    k = np.arange(half + 1, dtype=np.int64)[:, None] * t[None, :] % samples
    angle = np.arange(samples, dtype=np.float64) * (2.0 * math.pi / samples)
    cosine = np.cos(angle).astype(np.float32).astype(ml_dtypes.bfloat16)[k]
    sine = np.sin(angle).astype(np.float32).astype(ml_dtypes.bfloat16)[k]
    rest = np.zeros((14, samples // 4), ml_dtypes.bfloat16)
    return np.concatenate([cosine[:half], sine[:half], cosine[half:], sine[half:], rest])


def whole():
    return pl.BlockSpec(memory_space=pltpu.VMEM)


def by_baseline(visibilities):
    times, baselines, width = visibilities.shape
    half, tile, block = baselines // 2, 16, 16
    blocks = times // block

    def kernel(in_ref, out_ref, near, turned, in_sems, out_sems):
        def fetch(i):
            at = pl.ds(i * block, block)
            return pltpu.make_async_copy(in_ref.at[at], near.at[at], in_sems.at[i])

        def store(i):
            at = pl.ds(i * block, block)
            return pltpu.make_async_copy(
                turned.at[:, at, :], out_ref.at[:, at, :], out_sems.at[i]
            )

        for i in range(blocks):
            fetch(i).start()
        for i in range(blocks):
            fetch(i).wait()
            for t in range(i * block, (i + 1) * block, tile):
                for b in range(0, baselines, tile):
                    rows = jnp.swapaxes(near[t : t + tile, b : b + tile, :], 0, 1)
                    h, d = divmod(b, half)
                    turned[d : d + tile, t : t + tile, h * width : (h + 1) * width] = rows
            store(i).start()
        for i in range(blocks):
            store(i).wait()

    out = (half, times, 2 * width)
    return pl.pallas_call(
        kernel,
        in_specs=[pl.BlockSpec(memory_space=pl.ANY)],
        out_specs=pl.BlockSpec(memory_space=pl.ANY),
        out_shape=jax.ShapeDtypeStruct(out, jnp.bfloat16),
        scratch_shapes=[
            pltpu.VMEM(visibilities.shape, jnp.bfloat16),
            pltpu.VMEM(out, jnp.bfloat16),
            pltpu.SemaphoreType.DMA((blocks,)),
            pltpu.SemaphoreType.DMA((blocks,)),
        ],
        compiler_params=pltpu.CompilerParams(vmem_limit_bytes=56 * MIB),
        cost_estimate=pl.CostEstimate(
            flops=0, bytes_accessed=4 * visibilities.size, transcendentals=0
        ),
        name="by_baseline",
    )(visibilities)


def prepare(blocks, after):
    each_m, baselines, width = blocks[0].shape
    harm, peers = width // 2, len(blocks)
    depth = 2 * peers * baselines

    def kernel(*refs):
        block_refs, inverse_ref = refs[:peers], refs[peers + 1]
        for m in range(each_m):
            for part in range(2):
                at = slice(part * harm, (part + 1) * harm)
                for p in range(0, peers, 2):
                    two = [block_refs[p + i][m, :, at] for i in range(2)]
                    to = (part * peers + p) * baselines
                    inverse_ref[m, :, to : to + 2 * baselines] = jnp.concatenate(two, axis=0).T

    return pl.pallas_call(
        kernel,
        in_specs=[whole()] * peers + [pl.BlockSpec(memory_space=pl.ANY)],
        out_specs=whole(),
        out_shape=pltpu.VMEM((each_m, harm, depth), jnp.bfloat16),
        compiler_params=pltpu.CompilerParams(vmem_limit_bytes=56 * MIB),
        cost_estimate=pl.CostEstimate(
            flops=0, bytes_accessed=4 * each_m * harm * depth, transcendentals=0
        ),
        name="prepare",
    )(*blocks, after)


def transform(data, modes, ns):
    samples, width = data.shape
    per_b = width // (2 * ns)
    quarter, half = samples // 4, modes // 2
    scale = 1.0 / math.sqrt(samples)
    table = tables(modes, samples)

    def turn(v):
        parts = []
        for b in range(0, width, 2 * ns):
            parts += [v[:, b + ns : b + 2 * ns], -v[:, b : b + ns]]
        return jnp.concatenate(parts, axis=1)

    def kernel(table_ref, data_ref, out_ref, wide):
        z = [
            jnp.dot(
                table_ref[...],
                data_ref[j * quarter : (j + 1) * quarter, :],
                preferred_element_type=jnp.float32,
            )
            for j in range(4)
        ]
        c = [v[:half] for v in z]
        s = [v[half : 2 * half] for v in z]
        row = lax.broadcasted_iota(jnp.int32, (half, width), 0)
        odd = row % 2 == 1
        sign = jnp.where(odd, -1.0, 1.0)
        late = jnp.where(row % 4 >= 2, -1.0, 1.0)
        p_c, p_s = c[1] + sign * c[3], s[1] + sign * s[3]
        u = c[0] + sign * c[2] + late * jnp.where(odd, -p_s, p_c)
        v = turn(s[0] + sign * s[2] + late * jnp.where(odd, p_c, p_s))
        plus, minus = (u + v) * scale, (u - v) * scale
        last = z[0][2 * half :] + z[1][2 * half :] + z[2][2 * half :] + z[3][2 * half :]
        last = (last[0:1] - turn(last[1:2])) * scale
        minus = jnp.where(row == 0, last, minus).astype(jnp.bfloat16)
        both = sum(lax.broadcasted_iota(jnp.int32, (half, half), d) for d in (0, 1))
        back = jnp.where(both % half == 0, 1.0, 0.0).astype(jnp.bfloat16)
        minus = jnp.dot(back, minus, preferred_element_type=jnp.float32)
        for i, value in enumerate((minus, plus)):
            for b in range(per_b):
                to = pl.ds(i * half * per_b + b, half, stride=per_b)
                wide[to, :] = value[:, b * 2 * ns : (b + 1) * 2 * ns]
        out_ref[...] = wide[...].astype(jnp.bfloat16)

    return pl.pallas_call(
        kernel,
        in_specs=[whole()] * 2,
        out_specs=whole(),
        out_shape=jax.ShapeDtypeStruct((modes * per_b, 2 * ns), jnp.bfloat16),
        scratch_shapes=[pltpu.VMEM((modes * per_b, 2 * ns), jnp.float32)],
        compiler_params=pltpu.CompilerParams(vmem_limit_bytes=12 * MIB),
        cost_estimate=pl.CostEstimate(
            flops=2 * table.size * 4 * width,
            bytes_accessed=2 * table.size + 2 * data.size,
            transcendentals=0,
        ),
        name="transform",
    )(table, data)


def product(inverse, rows, sources, devices, ns):
    each_m, harm, _ = inverse.shape
    n_rows, width = rows.shape
    peers, per_b = sources.shape[0], 2
    step = peers * each_m * per_b
    outer = n_rows // step
    per = harm // devices

    def kernel(sources_ref, rows_ref, inverse_ref, out_ref, wide):
        wide[...] = rows_ref[...].astype(jnp.float32)
        for m in range(each_m):
            plain, turned = [], []
            for p in range(peers):
                for b in range(per_b):
                    start = (sources_ref[p] * each_m + m) * per_b + b
                    one = wide[pl.ds(start, outer, stride=step), :]
                    plain.append(one)
                    turned.append(jnp.concatenate([-one[:, ns:], one[:, :ns]], axis=1))
            weights = jnp.concatenate(plain + turned, axis=0).astype(jnp.bfloat16)
            sky = jnp.dot(inverse_ref[m], weights, preferred_element_type=jnp.float32)
            out_ref[:, m] = sky.astype(jnp.bfloat16).reshape(devices, per, 2 * ns)

    return pl.pallas_call(
        kernel,
        in_specs=[
            pl.BlockSpec(memory_space=pltpu.SMEM),
            whole(),
            whole(),
        ],
        out_specs=whole(),
        out_shape=jax.ShapeDtypeStruct((devices, each_m, per, 2 * ns), jnp.bfloat16),
        scratch_shapes=[
            pltpu.VMEM((n_rows, width), jnp.float32),
        ],
        compiler_params=pltpu.CompilerParams(vmem_limit_bytes=12 * MIB),
        cost_estimate=pl.CostEstimate(
            flops=4 * inverse.size * ns, bytes_accessed=2 * inverse.size, transcendentals=0
        ),
        name="product",
    )(sources, rows, inverse)


def per_device(visibilities, pseudo_inverse, baseline_group, group_count):
    tm, nx, nh, nc = (lax.axis_size(a) for a in ("tm", "x", "h", "c"))
    peers = nx * nc
    x, c = lax.axis_index("x"), lax.axis_index("c")
    local_t, local_b, width = visibilities.shape
    samples = local_t * tm
    mine_m = group_count.shape[0]
    modes = mine_m * tm
    each_m = mine_m // peers
    ns = width // 2

    data = by_baseline(visibilities)
    data = lax.all_to_all(data, "tm", split_axis=0, concat_axis=0, tiled=True)
    data = data.reshape(samples, 2 * width)

    active = (baseline_group[None, :] < group_count[:, None]).astype(jnp.bfloat16)
    masked = pseudo_inverse * active[:, :, None]
    blocks, sources = [], []
    for dx in range(nx):
        for dc in range(nc):
            to = (x + dx) % nx * nc + (c + dc) % nc
            block = lax.dynamic_slice_in_dim(masked, to * each_m, each_m, 0)
            if dx or dc:
                moves = [
                    (i, (i // nc + dx) % nx * nc + (i % nc + dc) % nc) for i in range(peers)
                ]
                block = lax.ppermute(block, ("x", "c"), moves)
            blocks.append(block)
            sources.append((x - dx) % nx * nc + (c - dc) % nc)
    data, *blocks = lax.optimization_barrier((data, *blocks))
    rows = transform(data, modes, ns)
    inverse = prepare(blocks, rows)

    rows = lax.all_to_all(rows, ("tm", "x", "c"), split_axis=0, concat_axis=0, tiled=True)
    sky = product(inverse, rows, jnp.stack(sources), nx * nh * nc, ns)

    sky = lax.all_to_all(sky, ("x", "h", "c"), split_axis=0, concat_axis=0, tiled=True)
    sky = sky.reshape(nx, nh, nc, each_m, -1, width).astype(jnp.float32).sum(axis=1)
    return sky.reshape(mine_m, -1, width).astype(jnp.bfloat16)


def solution(mesh):
    tm, base = mesh.devices.shape
    fine = Mesh(mesh.devices.reshape(tm, base // 4, 2, 2), ("tm", "x", "h", "c"))
    b = ("x", "h", "c")
    in_specs = (P("tm", b, None), P("tm", b, None), P(b), P("tm"))
    return jax.shard_map(
        per_device, mesh=fine, in_specs=in_specs, out_specs=P("tm", b, None), check_vma=False
    )
```
